32 devices in a mesh: net: 4 (over z), seg: 2 (over y), corner: 4 (over x, core).
Axes of the slice: x: 2, y: 2, z: 4, core: 2. Of those that a mesh axis runs over, the one named last changes fastest.
Arguments:
- tile_values: bfloat16 [512, 128, 1024], P(('net', 'seg', 'corner')), may hold values from -48 to 48
- tile_coords: int32 [512, 3], P(('net', 'seg', 'corner')), may hold values from 0 to 31, as said below
- tile_count: int32 [32], P(('net', 'seg', 'corner')), may hold values from 12 to 16, as said below
- owner_map: int32 [32], P('net'), may hold values from 0 to 31, as said below
- corner_factor: bfloat16 [64, 256], P('corner')
- seg_factor: bfloat16 [4096, 256], P(('seg', 'net'))
Outputs:
- net_factor: float32 [4096, 256], P(('net', 'seg', 'corner'))
The draws below stay inside these ranges and needn't reach their ends.
Inputs may be any that keep to these rules, and one draw needn't show every extreme that they name: `tile_coords`: row t of device d gives a corner block within the corner range stored by d's corner index, a net block that owner_map assigns to an owner slot of d's net index, and a segment block within the segment range of d's seg index. Among a device's 16 rows at most 4 name segment blocks stored by any one device of the net axis, and on every device two live rows name segment blocks stored by the same device of the net axis. The first tile_count[d] rows of device d are live; the others are ignored. `owner_map`: A permutation of the 32 net blocks.
All inputs are finite; a program needn't handle non-finite values.
Results may differ from the reference program's by a relative error of at most 0.0058.
The reference program's roundings to bfloat16 on the way (of `khatri`) count: a program that leaves them out, or rounds other values in their place, can miss the bound.
Values may be sent and summed in bfloat16 or wider, within the bound.
A program may use at most 64 MiB of HBM per device.

```python
import math
import jax
import jax.numpy as jnp
from jax import lax

R = 256
CORNERS = 64
CBLK = 8
NETB = 128
SEGB = 128
TILES_DEV = 16
BPH = 4
CAP = 4
GROUP = 8
NBLK = 32
SEGS = 4096
N_NET = 4
N_SEG = 2
N_CORNER = 4


def layout(key):
    key_owner, key_count, key_full, key_chosen, key_devices = jax.random.split(key, 5)
    owners = jax.random.permutation(key_owner, NBLK).astype(jnp.int32)
    device_ids = jnp.arange(NBLK, dtype=jnp.int32)
    lowest = max(2, 3 * TILES_DEV // 4)
    highest = max(lowest, TILES_DEV)
    counts = jax.random.randint(key_count, (NBLK,), lowest, highest + 1)
    heavy = jax.random.randint(key_full, (NBLK,), 0, 8) == 0
    chosen = jax.random.randint(key_chosen, (), 0, NBLK)
    light = (chosen + 1) % NBLK
    counts = jnp.where(heavy | (device_ids == chosen), TILES_DEV, counts)
    counts = jnp.where(device_ids == light, lowest, counts).astype(jnp.int32)
    corner_span = CORNERS // CBLK // N_CORNER

    def device_tiles(device_key, device, count):
        net_index = device // GROUP
        seg_index = device // N_CORNER % N_SEG
        corner_index = device % N_CORNER
        key_corner, key_net, key_slots, key_within, key_order = jax.random.split(device_key, 5)
        corner = corner_index * corner_span + jax.random.randint(key_corner, (TILES_DEV,), 0, corner_span)
        net_block = owners[net_index * GROUP + jax.random.randint(key_net, (TILES_DEV,), 0, GROUP)]
        slots = jax.random.permutation(key_slots, N_NET * CAP).astype(jnp.int32)
        partner = jnp.bitwise_xor(slots[0], 1)
        positions = jnp.arange(N_NET * CAP, dtype=jnp.int32)
        sort_keys = jnp.where(slots == partner, 1, 2 * positions)
        ordered = slots[jnp.argsort(sort_keys, stable=True)][:TILES_DEV]
        holder = ordered // CAP
        within = jax.random.randint(key_within, (TILES_DEV,), 0, BPH)
        segment = seg_index * BPH * N_NET + holder * BPH + within
        tile_ids = jnp.arange(TILES_DEV, dtype=jnp.int32)
        shuffle = jax.random.permutation(key_order, TILES_DEV).astype(jnp.int32)
        order_keys = jnp.where(tile_ids < count, shuffle, TILES_DEV + tile_ids)
        order = jnp.argsort(order_keys, stable=True)
        coords = jnp.stack([corner, net_block, segment], axis=1).astype(jnp.int32)
        return coords[order]
    device_keys = jax.vmap(lambda device: jax.random.fold_in(key_devices, device))(device_ids)
    coords = jax.vmap(device_tiles)(device_keys, device_ids, counts)
    return (owners, counts, coords.reshape(NBLK * TILES_DEV, 3))


def draw_tile_coords(key, part):
    owners, counts, coords = layout(jax.random.fold_in(key, 11))
    return coords


def draw_tile_count(key, part):
    owners, counts, coords = layout(jax.random.fold_in(key, 11))
    return counts


def draw_owner_map(key, part):
    owners, counts, coords = layout(jax.random.fold_in(key, 11))
    return owners


def draw_corner_factor(key, part):
    key_rows, key_base, key_cols = jax.random.split(key, 3)
    row_pos = jnp.arange(CORNERS, dtype=jnp.float32) / (CORNERS - 1)
    rising = (1.0 + 2.0 * row_pos)[:, None]
    spread = jnp.exp(jax.random.uniform(key_rows, (CORNERS, 1), minval=0.0, maxval=math.log(10.0)))
    base = jax.random.normal(key_base, (CORNERS, R))
    cols = jnp.exp(jax.random.uniform(key_cols, (1, R), minval=0.0, maxval=math.log(2.0)))
    scaled = base * spread * rising * cols / math.sqrt(CORNERS * 30.0)
    return scaled.astype(jnp.bfloat16)


def draw_seg_factor(key, part):
    key_rows, key_base, key_cols = jax.random.split(key, 3)
    row_pos = jnp.arange(SEGS, dtype=jnp.float32) / (SEGS - 1)
    rising = (1.0 + 2.0 * row_pos)[:, None]
    spread = jnp.exp(jax.random.uniform(key_rows, (SEGS, 1), minval=0.0, maxval=math.log(10.0)))
    base = jax.random.uniform(key_base, (SEGS, R), minval=0.2, maxval=1.0)
    cols = jnp.exp(jax.random.uniform(key_cols, (1, R), minval=0.0, maxval=math.log(2.0)))
    scaled = base * spread * rising * cols / math.sqrt(SEGS * 30.0)
    return scaled.astype(jnp.bfloat16)


def levels(stream_key, shape, cuts, smallest, largest):
    factor_of = 1.0
    for axis_at, blocks in cuts:
        steps = jax.random.uniform(jax.random.fold_in(jax.random.fold_in(stream_key, 6), axis_at), (blocks,), jnp.float32, smallest / len(cuts), largest / len(cuts))
        factor_of = factor_of * jnp.repeat(jnp.exp(steps), shape[axis_at] // blocks).reshape((-1,) + (1,) * (len(shape) - 1 - axis_at))
    return factor_of


def bell_draw(stream_key, dims, width, bound, pieces=(), kind=jnp.bfloat16):
    level = levels(stream_key, dims, pieces, -0.22, 0.18) if pieces else 1.0
    entries = jax.random.normal(stream_key, dims, jnp.float32) * width * level
    return jnp.minimum(jnp.maximum(entries, -bound), bound).astype(kind)


def setup_inputs(seed: int = 0) -> dict:
    key_of = jax.random.split(jax.random.key(seed), 7)
    tile_values = bell_draw(key_of[0], (NBLK * TILES_DEV, NETB, CBLK * SEGB), 8.0, 48.0, ((0, 32),))
    tile_coords = draw_tile_coords(jax.random.fold_in(key_of[6], 71), 0)
    tile_count = draw_tile_count(jax.random.fold_in(key_of[6], 71), 0)
    owner_map = draw_owner_map(jax.random.fold_in(key_of[6], 71), 0)
    corner_factor = draw_corner_factor(jax.random.fold_in(key_of[6], 71), 0)
    seg_factor = draw_seg_factor(jax.random.fold_in(key_of[6], 71), 0)
    return {"tile_values": tile_values, "tile_coords": tile_coords, "tile_count": tile_count, "owner_map": owner_map, "corner_factor": corner_factor, "seg_factor": seg_factor}


def solve_rows(gram, mttkrp):
    cholesky_low = jnp.linalg.cholesky(gram)
    forward = lax.linalg.triangular_solve(cholesky_low, mttkrp.T, left_side=True, lower=True)
    backward = lax.linalg.triangular_solve(cholesky_low, forward, left_side=True, lower=True, transpose_a=True)
    return backward.T

def reference(tile_values, tile_coords, tile_count, owner_map, corner_factor, seg_factor):
    live_mask = (jnp.arange(TILES_DEV)[None, :] < tile_count[:, None]).reshape(-1)
    owner_slot = jnp.zeros((NBLK,), jnp.int32).at[owner_map].set(jnp.arange(NBLK, dtype=jnp.int32))
    corner_blocks = corner_factor.reshape(CORNERS // CBLK, CBLK, R)
    seg_blocks = seg_factor.reshape(SEGS // SEGB, SEGB, R)

    def add_tile(total, packed):
        values, coords, live = packed
        corner_rows = lax.dynamic_index_in_dim(corner_blocks, coords[0].astype(jnp.int32), 0, keepdims=False).astype(jnp.float32)
        seg_rows = lax.dynamic_index_in_dim(seg_blocks, coords[2].astype(jnp.int32), 0, keepdims=False).astype(jnp.float32)
        khatri = (corner_rows[:, None, :] * seg_rows[None, :, :]).astype(jnp.bfloat16)
        khatri = lax.optimization_barrier(khatri)
        khatri = khatri.reshape(CBLK * SEGB, R).astype(jnp.float32)
        term = jnp.dot(values.astype(jnp.float32), khatri, precision=lax.Precision.HIGHEST)
        term = jnp.where(live, term, jnp.zeros_like(term))
        start = (owner_slot[coords[1]] * NETB).astype(jnp.int32)
        former = lax.dynamic_slice_in_dim(total, start, NETB, 0)
        return (lax.dynamic_update_slice_in_dim(total, former + term, start, 0), None)
    mttkrp, _ = lax.scan(add_tile, jnp.zeros((NBLK * NETB, R), jnp.float32), (tile_values, tile_coords, live_mask))
    corner_gram = jnp.dot(corner_factor.T.astype(jnp.float32), corner_factor.astype(jnp.float32), preferred_element_type=jnp.float32)
    seg_gram = jnp.dot(seg_factor.T.astype(jnp.float32), seg_factor.astype(jnp.float32), preferred_element_type=jnp.float32)
    return solve_rows(corner_gram * seg_gram, mttkrp)
```

```python
import functools

import jax
import jax.numpy as jnp
from jax import lax
from jax.experimental import pallas as pl
from jax.experimental.pallas import tpu as pltpu
from jax.sharding import PartitionSpec as P

CBLK = 8
MESH = pl.DeviceIdType.MESH
HIGH = lax.Precision.HIGHEST
PAIR = 2


def dot32(a, b, dims=((1,), (0,))):
    return lax.dot_general(a, b, (dims, ((), ())), precision=HIGH, preferred_element_type=jnp.float32)


def invert(s):
    n = s.shape[0]
    row = lax.broadcasted_iota(jnp.int32, (n, 1), 0)
    col = lax.broadcasted_iota(jnp.int32, (1, n), 1)
    for k in range(0, n, 2):
        r0, r1 = s[k : k + 1, :], s[k + 1 : k + 2, :]
        c0, c1 = s[:, k : k + 1], s[:, k + 1 : k + 2]
        a, b, d = r0[:, k : k + 1], r0[:, k + 1 : k + 2], r1[:, k + 1 : k + 2]
        scale = 1.0 / (a * d - b * b)
        r0 = r0 - (col == k).astype(jnp.float32)
        r1 = r1 - (col == k + 1).astype(jnp.float32)
        c0 = c0 - (row == k).astype(jnp.float32)
        c1 = c1 - (row == k + 1).astype(jnp.float32)
        u0 = (d * scale) * r0 - (b * scale) * r1
        u1 = (a * scale) * r1 - (b * scale) * r0
        s = s - c0 * u0 - c1 * u1
    return jnp.where(row == col, 2.0, 0.0) - s


def kernel(
    nn, ns, nc, coords, count, owner, corner_ref, seg_ref, values_ref, out_ref,
    gathered, corner_all, corner_wide, values, partial, gram_in, gram_own, gram_all,
    summed, pair_in, rows_in, square, upper, local_sem, z_send, z_recv, c_send, c_recv,
    h_send, h_recv, l_send, l_recv, g_send, g_recv, p_send, p_recv, s_send, s_recv,
):
    net, seg, corner = lax.axis_index("net"), lax.axis_index("seg"), lax.axis_index("corner")
    highs = nc // PAIR
    high, low = corner // PAIR, lax.rem(corner, PAIR)
    other_low = high * PAIR + 1 - low
    group = ns * nc
    pairs = group // PAIR
    slot = seg * nc + corner
    mine = seg * highs + high
    slots = values.shape[0]
    columns = corner_ref.shape[1]
    half = columns // 2
    held = gathered.shape[0] // nn
    chunk = held // nc
    net_rows = values.shape[1]

    def remote(src, dst, send, recv, **where):
        return pltpu.make_async_remote_copy(
            src_ref=src, dst_ref=dst, send_sem=send, recv_sem=recv, device_id=where, device_id_type=MESH
        )

    parts = local_sem.shape[0] - 1
    step = slots // parts
    loads = [
        pltpu.make_async_copy(
            values_ref.at[pl.ds(i * step, step)], values.at[pl.ds(i * step, step)], local_sem.at[i]
        )
        for i in range(parts)
    ]
    own_seg = pltpu.make_async_copy(seg_ref, gathered.at[pl.ds(net * held, held)], local_sem.at[parts])
    own_seg.start()
    for load in loads:
        load.start()

    barrier = pltpu.get_barrier_semaphore()
    for i in range(1, group):
        peer = lax.rem(slot + i, group)
        pl.semaphore_signal(
            barrier, inc=1, device_id={"seg": peer // nc, "corner": lax.rem(peer, nc)}, device_id_type=MESH
        )
    for i in range(1, nn):
        pl.semaphore_signal(barrier, inc=1, device_id={"net": lax.rem(net + i, nn)}, device_id_type=MESH)
    pl.semaphore_wait(barrier, group + nn - 2)

    def block(source, which):
        return pl.ds(source * held + which * chunk, chunk)

    sends = []

    def go(copy):
        copy.start()
        sends.append(copy)

    for i in range(1, nn):
        go(
            remote(
                seg_ref.at[pl.ds(corner * chunk, chunk)], gathered.at[block(net, corner)],
                z_send.at[i - 1], z_recv.at[i - 1], net=lax.rem(net + i, nn),
            )
        )
    for i in range(1, nc):
        go(
            remote(
                corner_ref, corner_all.at[corner], c_send.at[i - 1], c_recv.at[i - 1],
                corner=lax.rem(corner + i, nc),
            )
        )
    corner_all[pl.ds(corner, 1)] = corner_ref[...][None]
    corner_wide[...] = corner_ref[...].astype(jnp.float32).reshape(corner_wide.shape)

    def gram_of(source):
        rows = gathered[pl.ds(source * held, held)].reshape(-1, columns)
        left = gathered[pl.ds(source * held, held), :, pl.ds(pl.multiple_of(low * half, half), half)]
        return lax.dot_general(
            left.reshape(-1, half), rows, (((0,), (0,)), ((), ())), preferred_element_type=jnp.float32
        )

    own_seg.wait()
    gram_own[...] = gram_of(net)

    for i in range(1, nn):
        source = lax.rem(net - i + nn, nn)
        got = gathered.at[block(source, corner)]
        remote(got, got, z_send.at[i - 1], z_recv.at[i - 1], net=source).wait_recv()
        for j in range(1, highs):
            at = (i - 1) * (highs - 1) + j - 1
            go(
                remote(
                    got, got, h_send.at[at], h_recv.at[at], corner=lax.rem(high + j, highs) * PAIR + low
                )
            )
        at = (i - 1) * highs
        go(remote(got, got, l_send.at[at], l_recv.at[at], corner=other_low))
    for i in range(1, nn):
        source = lax.rem(net - i + nn, nn)
        for j in range(1, highs):
            at = (i - 1) * (highs - 1) + j - 1
            got = gathered.at[block(source, lax.rem(high - j + highs, highs) * PAIR + low)]
            remote(got, got, h_send.at[at], h_recv.at[at], corner=other_low).wait_recv()
            to = (i - 1) * highs + j
            go(remote(got, got, l_send.at[to], l_recv.at[to], corner=other_low))
    for i in range(1, nn):
        source = lax.rem(net - i + nn, nn)
        for j in range(highs):
            at = (i - 1) * highs + j
            got = gathered.at[block(source, lax.rem(high - j + highs, highs) * PAIR + 1 - low)]
            remote(got, got, l_send.at[at], l_recv.at[at], corner=other_low).wait_recv()
        gram_own[...] += gram_of(source)

    for j in range(1, ns):
        go(
            remote(
                gram_own, gram_in.at[j - 1], g_send.at[j - 1], g_recv.at[j - 1], seg=lax.rem(seg + j, ns)
            )
        )
    for load in loads:
        load.wait()

    corner_span, seg_span = corner_ref.shape[0] // CBLK, held * nn

    def tile(t, carry):
        corner_rows = corner_wide[lax.rem(coords[t, 0], corner_span)]
        seg_rows = gathered[lax.rem(coords[t, 2], seg_span)].astype(jnp.float32)
        khatri = jnp.concatenate(
            [(corner_rows[a : a + 1, :] * seg_rows).astype(jnp.bfloat16) for a in range(CBLK)], axis=0
        )
        partial[t] = jnp.dot(values[t], khatri, preferred_element_type=jnp.float32)
        return carry

    lax.fori_loop(0, slots // 2, tile, 0)

    total = gram_own[...]
    for j in range(1, ns):
        remote(
            gram_own, gram_in.at[j - 1], g_send.at[j - 1], g_recv.at[j - 1], seg=lax.rem(seg + j, ns)
        ).wait_recv()
        total = total + gram_in[j - 1]
    gram_all[pl.ds(low, 1)] = total[None]
    go(
        remote(
            gram_all.at[low], gram_all.at[low], g_send.at[ns - 1], g_recv.at[ns - 1], corner=other_low
        )
    )

    lax.fori_loop(slots // 2, slots, tile, 0)

    live = count[0]

    def add_up(q):
        block_of = owner[q]
        acc = jnp.zeros((net_rows, columns), jnp.float32)
        for t in range(slots):
            take = jnp.logical_and(coords[t, 1] == block_of, t < live)
            acc = acc + jnp.where(take, partial[t], 0.0)
        return acc

    def pair_copy(h):
        return remote(
            summed.at[h * PAIR + 1 - low], pair_in.at[h], p_send.at[h], p_recv.at[h], corner=other_low
        )

    def give(h, carry):
        summed[pl.ds(h * PAIR + 1 - low, 1)] = add_up(h * PAIR + 1 - low)[None]
        pair_copy(h).start()
        return carry

    def keep(h, carry):
        summed[pl.ds(h * PAIR + low, 1)] = add_up(h * PAIR + low)[None]
        return carry

    lax.fori_loop(0, pairs, give, 0)
    lax.fori_loop(0, pairs, keep, 0)

    def row_copy(i):
        h = lax.rem(mine + i, pairs)
        return remote(
            summed.at[h * PAIR + low], rows_in.at[i - 1], s_send.at[i - 1], s_recv.at[i - 1],
            seg=h // highs, corner=lax.rem(h, highs) * PAIR + low,
        )

    def pass_on(i, carry):
        h = lax.rem(mine + i, pairs)
        got = pair_in.at[h]
        remote(got, got, p_send.at[h], p_recv.at[h], corner=other_low).wait_recv()
        at = h * PAIR + low
        summed[pl.ds(at, 1)] = summed[pl.ds(at, 1)] + pair_in[pl.ds(h, 1)]

        @pl.when(i < pairs)
        def _():
            row_copy(i).start()

        return carry

    lax.fori_loop(1, pairs + 1, pass_on, 0)

    for i in range(1, nc):
        remote(
            corner_ref, corner_all.at[lax.rem(corner - i + nc, nc)], c_send.at[i - 1], c_recv.at[i - 1],
            corner=lax.rem(corner + i, nc),
        ).wait_recv()
    remote(
        gram_all.at[low], gram_all.at[1 - low], g_send.at[ns - 1], g_recv.at[ns - 1], corner=other_low
    ).wait_recv()
    factor = corner_all[...].reshape(-1, columns)
    gram = lax.dot_general(factor, factor, (((0,), (0,)), ((), ())), preferred_element_type=jnp.float32)
    gram = gram * gram_all[...].reshape(columns, columns)
    row = lax.broadcasted_iota(jnp.int32, (columns, 1), 0)
    col = lax.broadcasted_iota(jnp.int32, (1, columns), 1)
    diag = jnp.where(row == col, gram, 0.0)
    scale_row = lax.rsqrt(jnp.sum(diag, axis=0, keepdims=True))
    scale_col = lax.rsqrt(jnp.sum(diag, axis=1, keepdims=True))
    gram = gram * scale_col * scale_row
    square[0] = gram[:half, :half]
    square[1] = gram[half:, half:]
    upper[0] = gram[:half, half:]

    def halves(h, carry):
        square[h] = invert(square[h])

        @pl.when(h == 0)
        def _():
            upper[1] = dot32(square[0], upper[0])
            square[1] = square[1] - dot32(upper[0], upper[1], ((0,), (0,)))

        return carry

    lax.fori_loop(0, 2, halves, 0)

    def take_rows(i, acc):
        row_copy(i).wait_recv()
        return acc + rows_in[i - 1]

    mttkrp = lax.fori_loop(1, pairs, take_rows, summed[slot]) * scale_row
    first, second = mttkrp[:, :half], mttkrp[:, half:]
    second = dot32(second - dot32(first, upper[1]), square[1])
    first = dot32(first - dot32(second, upper[0], ((1,), (1,))), square[0])
    out_ref[:, :half] = first * scale_row[:, :half]
    out_ref[:, half:] = second * scale_row[:, half:]

    for copy in sends:
        copy.wait_send()

    def end_pair(h, carry):
        pair_copy(h).wait_send()
        return carry

    def end_row(i, carry):
        row_copy(i).wait_send()
        return carry

    lax.fori_loop(0, pairs, end_pair, 0)
    lax.fori_loop(1, pairs, end_row, 0)


def body(tile_values, tile_coords, tile_count, owner_map, corner_factor, seg_factor):
    nn, ns, nc = lax.axis_size("net"), lax.axis_size("seg"), lax.axis_size("corner")
    slots, net_rows, depth = tile_values.shape
    columns = corner_factor.shape[1]
    width = depth // CBLK
    held = seg_factor.shape[0] // width
    group = ns * nc
    pairs, highs, half = group // PAIR, nc // PAIR, columns // 2
    smem = pl.BlockSpec(memory_space=pltpu.SMEM)
    vmem = pl.BlockSpec(memory_space=pltpu.VMEM)
    hbm = pl.BlockSpec(memory_space=pl.ANY)
    dma = lambda n: pltpu.SemaphoreType.DMA((max(n, 1),))
    f32, bf16 = jnp.float32, jnp.bfloat16
    return pl.pallas_call(
        functools.partial(kernel, nn, ns, nc),
        out_shape=jax.ShapeDtypeStruct((net_rows, columns), f32),
        in_specs=[smem, smem, smem, vmem, hbm, hbm],
        out_specs=vmem,
        scratch_shapes=[
            pltpu.VMEM((nn * held, width, columns), bf16),
            pltpu.VMEM((nc,) + corner_factor.shape, bf16),
            pltpu.VMEM((corner_factor.shape[0] // CBLK, CBLK, columns), f32),
            pltpu.VMEM(tile_values.shape, bf16),
            pltpu.VMEM((slots, net_rows, columns), f32),
            pltpu.VMEM((max(ns - 1, 1), half, columns), f32),
            pltpu.VMEM((half, columns), f32),
            pltpu.VMEM((2, half, columns), f32),
            pltpu.VMEM((group, net_rows, columns), f32),
            pltpu.VMEM((pairs, net_rows, columns), f32),
            pltpu.VMEM((max(pairs - 1, 1), net_rows, columns), f32),
            pltpu.VMEM((2, half, half), f32),
            pltpu.VMEM((2, half, half), f32),
            dma(5),
            dma(nn - 1), dma(nn - 1), dma(nc - 1), dma(nc - 1),
            dma((nn - 1) * (highs - 1)), dma((nn - 1) * (highs - 1)),
            dma((nn - 1) * highs), dma((nn - 1) * highs),
            dma(ns), dma(ns), dma(pairs), dma(pairs), dma(pairs - 1), dma(pairs - 1),
        ],
        compiler_params=pltpu.CompilerParams(
            collective_id=0, has_side_effects=True, vmem_limit_bytes=48 * 1024 * 1024
        ),
    )(
        tile_coords, tile_count, owner_map, corner_factor,
        seg_factor.reshape(held, width, columns), tile_values,
    )


def solution(mesh):
    return jax.shard_map(
        body,
        mesh=mesh,
        in_specs=(
            P(("net", "seg", "corner"), None, None),
            P(("net", "seg", "corner"), None),
            P(("net", "seg", "corner")),
            P("net"),
            P("corner", None),
            P(("seg", "net"), None),
        ),
        out_specs=P(("net", "seg", "corner"), None),
        check_vma=False,
    )
```

```python
import functools

import jax
import jax.numpy as jnp
from jax import lax
from jax.experimental import pallas as pl
from jax.experimental.pallas import tpu as pltpu
from jax.sharding import PartitionSpec as P

CBLK = 8
MESH = pl.DeviceIdType.MESH
HIGH = lax.Precision.HIGHEST
PAIR = 2


def dot32(a, b, dims=((1,), (0,))):
    return lax.dot_general(a, b, (dims, ((), ())), precision=HIGH, preferred_element_type=jnp.float32)


def invert(s):
    n = s.shape[0]
    row = lax.broadcasted_iota(jnp.int32, (n, n), 0)
    col = lax.broadcasted_iota(jnp.int32, (n, n), 1)
    sub, lane = row[:8], col[:8]
    s = s.reshape(n // 8, 8, n)
    for k in range(0, n, 4):
        g, o = divmod(k, 8)
        cols = [jnp.broadcast_to(s[:, :, k + j : k + j + 1], s.shape) for j in range(4)]
        own = s[g]
        block = {
            (i, j): jnp.broadcast_to(cols[j][g][o + i : o + i + 1, :], (8, n))
            for i in range(4)
            for j in range(i, 4)
        }
        rows = [
            jnp.broadcast_to(own[o + i : o + i + 1, :], (8, n)) - jnp.where(lane == k + i, 1.0, 0.0)
            for i in range(4)
        ]
        scale = 1.0 / (block[0, 0] * block[1, 1] - block[0, 1] * block[0, 1])
        p00, p01, p11 = block[1, 1] * scale, -block[0, 1] * scale, block[0, 0] * scale
        v02 = p00 * block[0, 2] + p01 * block[1, 2]
        v03 = p00 * block[0, 3] + p01 * block[1, 3]
        v12 = p01 * block[0, 2] + p11 * block[1, 2]
        v13 = p01 * block[0, 3] + p11 * block[1, 3]
        c22 = block[2, 2] - (block[0, 2] * v02 + block[1, 2] * v12)
        c23 = block[2, 3] - (block[0, 2] * v03 + block[1, 2] * v13)
        c33 = block[3, 3] - (block[0, 3] * v03 + block[1, 3] * v13)
        scale = 1.0 / (c22 * c33 - c23 * c23)
        w0 = p00 * rows[0] + p01 * rows[1]
        w1 = p01 * rows[0] + p11 * rows[1]
        t2 = (rows[2] - (v02 * rows[0] + v12 * rows[1])) * scale
        t3 = (rows[3] - (v03 * rows[0] + v13 * rows[1])) * scale
        u2 = c33 * t2 - c23 * t3
        u3 = c22 * t3 - c23 * t2
        u0 = w0 - (v02 * u2 + v03 * u3)
        u1 = w1 - (v12 * u2 + v13 * u3)
        add = sum(jnp.where(sub == o + j, u, 0.0) for j, u in enumerate((u0, u1, u2, u3)))
        s = s - ((cols[0] * u0 + cols[1] * u1) + (cols[2] * u2 + cols[3] * u3))
        parts = [s[:g], (s[g] + add)[None], s[g + 1 :]]
        s = jnp.concatenate([part for part in parts if part.shape[0]], axis=0)
    return jnp.where(row == col, 2.0, 0.0) - s.reshape(n, n)


def kernel(
    nn, ns, nc, coords_ref, count_ref, owner_ref, corner_hbm, seg_ref, values_ref, out_ref,
    coords, count, owner, corner_ref,
    gathered, corner_all, corner_wide, values, partial, gram_in, gram_own, gram_all,
    summed, pair_in, rows_in, square, upper, local_sem, small_sem, z_send, z_recv, c_send, c_recv,
    h_send, h_recv, l_send, l_recv, g_send, g_recv, p_send, p_recv, s_send, s_recv,
):
    net, seg, corner = lax.axis_index("net"), lax.axis_index("seg"), lax.axis_index("corner")
    highs = nc // PAIR
    high, low = corner // PAIR, lax.rem(corner, PAIR)
    other_low = high * PAIR + 1 - low
    group = ns * nc
    pairs = group // PAIR
    slot = seg * nc + corner
    mine = seg * highs + high
    slots = values.shape[0]
    columns = corner_ref.shape[1]
    half = columns // 2
    held = gathered.shape[0] // nn
    chunk = held // nc
    net_rows = values.shape[1]

    def remote(src, dst, send, recv, **where):
        return pltpu.make_async_remote_copy(
            src_ref=src, dst_ref=dst, send_sem=send, recv_sem=recv, device_id=where, device_id_type=MESH
        )

    parts = local_sem.shape[0] - 1
    step = slots // parts
    loads = [
        pltpu.make_async_copy(
            values_ref.at[pl.ds(i * step, step)], values.at[pl.ds(i * step, step)], local_sem.at[i]
        )
        for i in range(parts)
    ]
    own_seg = pltpu.make_async_copy(seg_ref, gathered.at[pl.ds(net * held, held)], local_sem.at[parts])
    small = [
        pltpu.make_async_copy(source, to, small_sem.at[i])
        for i, (source, to) in enumerate(
            ((corner_hbm, corner_ref), (coords_ref, coords), (count_ref, count), (owner_ref, owner))
        )
    ]
    for copy in small:
        copy.start()
    own_seg.start()
    for load in loads:
        load.start()

    small[0].wait()
    barrier = pltpu.get_barrier_semaphore()
    for i in range(1, group):
        peer = lax.rem(slot + i, group)
        pl.semaphore_signal(
            barrier, inc=1, device_id={"seg": peer // nc, "corner": lax.rem(peer, nc)}, device_id_type=MESH
        )
    for i in range(1, nn):
        pl.semaphore_signal(barrier, inc=1, device_id={"net": lax.rem(net + i, nn)}, device_id_type=MESH)
    pl.semaphore_wait(barrier, group + nn - 2)

    def block(source, which):
        return pl.ds(source * held + which * chunk, chunk)

    sends = []

    def go(copy):
        copy.start()
        sends.append(copy)

    for i in range(1, nn):
        go(
            remote(
                seg_ref.at[pl.ds(corner * chunk, chunk)], gathered.at[block(net, corner)],
                z_send.at[i - 1], z_recv.at[i - 1], net=lax.rem(net + i, nn),
            )
        )
    for i in range(1, nc):
        go(
            remote(
                corner_ref, corner_all.at[corner], c_send.at[i - 1], c_recv.at[i - 1],
                corner=lax.rem(corner + i, nc),
            )
        )
    corner_all[pl.ds(corner, 1)] = corner_ref[...][None]
    corner_wide[...] = corner_ref[...].astype(jnp.float32).reshape(corner_wide.shape)

    def gram_of(source):
        rows = gathered[pl.ds(source * held, held)].reshape(-1, columns)
        left = gathered[pl.ds(source * held, held), :, pl.ds(pl.multiple_of(low * half, half), half)]
        return lax.dot_general(
            left.reshape(-1, half), rows, (((0,), (0,)), ((), ())), preferred_element_type=jnp.float32
        )

    own_seg.wait()
    gram_own[...] = gram_of(net)

    for i in range(1, nn):
        source = lax.rem(net - i + nn, nn)
        got = gathered.at[block(source, corner)]
        remote(got, got, z_send.at[i - 1], z_recv.at[i - 1], net=source).wait_recv()
        for j in range(1, highs):
            at = (i - 1) * (highs - 1) + j - 1
            go(
                remote(
                    got, got, h_send.at[at], h_recv.at[at], corner=lax.rem(high + j, highs) * PAIR + low
                )
            )
        at = (i - 1) * highs
        go(remote(got, got, l_send.at[at], l_recv.at[at], corner=other_low))
    for i in range(1, nn):
        source = lax.rem(net - i + nn, nn)
        for j in range(1, highs):
            at = (i - 1) * (highs - 1) + j - 1
            got = gathered.at[block(source, lax.rem(high - j + highs, highs) * PAIR + low)]
            remote(got, got, h_send.at[at], h_recv.at[at], corner=other_low).wait_recv()
            to = (i - 1) * highs + j
            go(remote(got, got, l_send.at[to], l_recv.at[to], corner=other_low))
    for i in range(1, nn):
        source = lax.rem(net - i + nn, nn)
        for j in range(highs):
            at = (i - 1) * highs + j
            got = gathered.at[block(source, lax.rem(high - j + highs, highs) * PAIR + 1 - low)]
            remote(got, got, l_send.at[at], l_recv.at[at], corner=other_low).wait_recv()
        gram_own[...] += gram_of(source)

    for j in range(1, ns):
        go(
            remote(
                gram_own, gram_in.at[j - 1], g_send.at[j - 1], g_recv.at[j - 1], seg=lax.rem(seg + j, ns)
            )
        )
    for load in loads + small[1:]:
        load.wait()

    corner_span, seg_span = corner_ref.shape[0] // CBLK, held * nn

    def tile(t, carry):
        corner_rows = corner_wide[lax.rem(coords[0, t], corner_span)]
        seg_rows = gathered[lax.rem(coords[2, t], seg_span)].astype(jnp.float32)
        khatri = jnp.concatenate(
            [(corner_rows[a : a + 1, :] * seg_rows).astype(jnp.bfloat16) for a in range(CBLK)], axis=0
        )
        partial[t] = jnp.dot(values[t], khatri, preferred_element_type=jnp.float32)
        return carry

    lax.fori_loop(0, slots // 2, tile, 0)

    total = gram_own[...]
    for j in range(1, ns):
        remote(
            gram_own, gram_in.at[j - 1], g_send.at[j - 1], g_recv.at[j - 1], seg=lax.rem(seg + j, ns)
        ).wait_recv()
        total = total + gram_in[j - 1]
    gram_all[pl.ds(low, 1)] = total[None]
    go(
        remote(
            gram_all.at[low], gram_all.at[low], g_send.at[ns - 1], g_recv.at[ns - 1], corner=other_low
        )
    )

    lax.fori_loop(slots // 2, slots, tile, 0)

    live = count[0]

    def add_up(q):
        block_of = owner[q]
        acc = jnp.zeros((net_rows, columns), jnp.float32)
        for t in range(slots):
            take = jnp.logical_and(coords[1, t] == block_of, t < live)
            acc = acc + jnp.where(take, partial[t], 0.0)
        return acc

    def pair_copy(h):
        return remote(
            summed.at[h * PAIR + 1 - low], pair_in.at[h], p_send.at[h], p_recv.at[h], corner=other_low
        )

    def give(h, carry):
        summed[pl.ds(h * PAIR + 1 - low, 1)] = add_up(h * PAIR + 1 - low)[None]
        pair_copy(h).start()
        return carry

    def keep(h, carry):
        summed[pl.ds(h * PAIR + low, 1)] = add_up(h * PAIR + low)[None]
        return carry

    lax.fori_loop(0, pairs, give, 0)
    lax.fori_loop(0, pairs, keep, 0)

    def row_copy(i):
        h = lax.rem(mine + i, pairs)
        return remote(
            summed.at[h * PAIR + low], rows_in.at[i - 1], s_send.at[i - 1], s_recv.at[i - 1],
            seg=h // highs, corner=lax.rem(h, highs) * PAIR + low,
        )

    def pass_on(i, carry):
        h = lax.rem(mine + i, pairs)
        got = pair_in.at[h]
        remote(got, got, p_send.at[h], p_recv.at[h], corner=other_low).wait_recv()
        at = h * PAIR + low
        summed[pl.ds(at, 1)] = summed[pl.ds(at, 1)] + pair_in[pl.ds(h, 1)]

        @pl.when(i < pairs)
        def _():
            row_copy(i).start()

        return carry

    lax.fori_loop(1, pairs + 1, pass_on, 0)

    for i in range(1, nc):
        remote(
            corner_ref, corner_all.at[lax.rem(corner - i + nc, nc)], c_send.at[i - 1], c_recv.at[i - 1],
            corner=lax.rem(corner + i, nc),
        ).wait_recv()
    remote(
        gram_all.at[low], gram_all.at[1 - low], g_send.at[ns - 1], g_recv.at[ns - 1], corner=other_low
    ).wait_recv()
    factor = corner_all[...].reshape(-1, columns)
    gram = lax.dot_general(factor, factor, (((0,), (0,)), ((), ())), preferred_element_type=jnp.float32)
    gram = gram * gram_all[...].reshape(columns, columns)
    row = lax.broadcasted_iota(jnp.int32, (columns, 1), 0)
    col = lax.broadcasted_iota(jnp.int32, (1, columns), 1)
    diag = jnp.where(row == col, gram, 0.0)
    scale_row = lax.rsqrt(jnp.sum(diag, axis=0, keepdims=True))
    scale_col = lax.rsqrt(jnp.sum(diag, axis=1, keepdims=True))
    gram = gram * scale_col * scale_row
    square[0] = gram[:half, :half]
    square[1] = gram[half:, half:]
    upper[0] = gram[:half, half:]

    def halves(h, carry):
        square[h] = invert(square[h])

        @pl.when(h == 0)
        def _():
            upper[1] = dot32(square[0], upper[0])
            square[1] = square[1] - dot32(upper[0], upper[1], ((0,), (0,)))

        return carry

    lax.fori_loop(0, 2, halves, 0)

    def take_rows(i, acc):
        row_copy(i).wait_recv()
        return acc + rows_in[i - 1]

    mttkrp = lax.fori_loop(1, pairs, take_rows, summed[slot]) * scale_row
    first, second = mttkrp[:, :half], mttkrp[:, half:]
    second = dot32(second - dot32(first, upper[1]), square[1])
    first = dot32(first - dot32(second, upper[0], ((1,), (1,))), square[0])
    out_ref[:, :half] = first * scale_row[:, :half]
    out_ref[:, half:] = second * scale_row[:, half:]

    for copy in sends:
        copy.wait_send()

    def end_pair(h, carry):
        pair_copy(h).wait_send()
        return carry

    def end_row(i, carry):
        row_copy(i).wait_send()
        return carry

    lax.fori_loop(0, pairs, end_pair, 0)
    lax.fori_loop(1, pairs, end_row, 0)


def body(tile_values, tile_coords, tile_count, owner_map, corner_factor, seg_factor):
    nn, ns, nc = lax.axis_size("net"), lax.axis_size("seg"), lax.axis_size("corner")
    slots, net_rows, depth = tile_values.shape
    columns = corner_factor.shape[1]
    width = depth // CBLK
    held = seg_factor.shape[0] // width
    group = ns * nc
    pairs, highs, half = group // PAIR, nc // PAIR, columns // 2
    vmem = pl.BlockSpec(memory_space=pltpu.VMEM)
    hbm = pl.BlockSpec(memory_space=pltpu.HBM)
    dma = lambda n: pltpu.SemaphoreType.DMA((max(n, 1),))
    f32, bf16 = jnp.float32, jnp.bfloat16
    return pl.pallas_call(
        functools.partial(kernel, nn, ns, nc),
        out_shape=jax.ShapeDtypeStruct((net_rows, columns), f32),
        in_specs=[hbm] * 6,
        out_specs=vmem,
        scratch_shapes=[
            pltpu.SMEM((3, slots), jnp.int32),
            pltpu.SMEM(tile_count.shape, jnp.int32),
            pltpu.SMEM(owner_map.shape, jnp.int32),
            pltpu.VMEM(corner_factor.shape, bf16),
            pltpu.VMEM((nn * held, width, columns), bf16),
            pltpu.VMEM((nc,) + corner_factor.shape, bf16),
            pltpu.VMEM((corner_factor.shape[0] // CBLK, CBLK, columns), f32),
            pltpu.VMEM(tile_values.shape, bf16),
            pltpu.VMEM((slots, net_rows, columns), f32),
            pltpu.VMEM((max(ns - 1, 1), half, columns), f32),
            pltpu.VMEM((half, columns), f32),
            pltpu.VMEM((2, half, columns), f32),
            pltpu.VMEM((group, net_rows, columns), f32),
            pltpu.VMEM((pairs, net_rows, columns), f32),
            pltpu.VMEM((max(pairs - 1, 1), net_rows, columns), f32),
            pltpu.VMEM((2, half, half), f32),
            pltpu.VMEM((2, half, half), f32),
            dma(5), dma(4),
            dma(nn - 1), dma(nn - 1), dma(nc - 1), dma(nc - 1),
            dma((nn - 1) * (highs - 1)), dma((nn - 1) * (highs - 1)),
            dma((nn - 1) * highs), dma((nn - 1) * highs),
            dma(ns), dma(ns), dma(pairs), dma(pairs), dma(pairs - 1), dma(pairs - 1),
        ],
        compiler_params=pltpu.CompilerParams(
            collective_id=0, has_side_effects=True, vmem_limit_bytes=63 * 1024 * 1024
        ),
    )(
        tile_coords.T, tile_count, owner_map, corner_factor,
        seg_factor.reshape(held, width, columns), tile_values,
    )


def solution(mesh):
    return jax.shard_map(
        body,
        mesh=mesh,
        in_specs=(
            P(("net", "seg", "corner"), None, None),
            P(("net", "seg", "corner"), None),
            P(("net", "seg", "corner")),
            P("net"),
            P("corner", None),
            P(("seg", "net"), None),
        ),
        out_specs=P(("net", "seg", "corner"), None),
        check_vma=False,
    )
```

```python
import functools

import jax
import jax.numpy as jnp
from jax import lax
from jax.experimental import pallas as pl
from jax.experimental.pallas import tpu as pltpu
from jax.sharding import PartitionSpec as P

CBLK = 8
MESH = pl.DeviceIdType.MESH
HIGH = lax.Precision.HIGHEST
PAIR = 2


def dot32(a, b, dims=((1,), (0,))):
    return lax.dot_general(a, b, (dims, ((), ())), precision=HIGH, preferred_element_type=jnp.float32)


def invert(s):
    n = s.shape[0]
    row = lax.broadcasted_iota(jnp.int32, (n, n), 0)
    col = lax.broadcasted_iota(jnp.int32, (n, n), 1)
    sub, lane = row[:8], col[:8]
    s = s.reshape(n // 8, 8, n)
    for k in range(0, n, 4):
        g, o = divmod(k, 8)
        cols = [jnp.broadcast_to(s[:, :, k + j : k + j + 1], s.shape) for j in range(4)]
        own = s[g]
        block = {
            (i, j): jnp.broadcast_to(cols[j][g][o + i : o + i + 1, :], (8, n))
            for i in range(4)
            for j in range(i, 4)
        }
        rows = [
            jnp.broadcast_to(own[o + i : o + i + 1, :], (8, n)) - jnp.where(lane == k + i, 1.0, 0.0)
            for i in range(4)
        ]
        scale = 1.0 / (block[0, 0] * block[1, 1] - block[0, 1] * block[0, 1])
        p00, p01, p11 = block[1, 1] * scale, -block[0, 1] * scale, block[0, 0] * scale
        v02 = p00 * block[0, 2] + p01 * block[1, 2]
        v03 = p00 * block[0, 3] + p01 * block[1, 3]
        v12 = p01 * block[0, 2] + p11 * block[1, 2]
        v13 = p01 * block[0, 3] + p11 * block[1, 3]
        c22 = block[2, 2] - (block[0, 2] * v02 + block[1, 2] * v12)
        c23 = block[2, 3] - (block[0, 2] * v03 + block[1, 2] * v13)
        c33 = block[3, 3] - (block[0, 3] * v03 + block[1, 3] * v13)
        scale = 1.0 / (c22 * c33 - c23 * c23)
        w0 = p00 * rows[0] + p01 * rows[1]
        w1 = p01 * rows[0] + p11 * rows[1]
        t2 = (rows[2] - (v02 * rows[0] + v12 * rows[1])) * scale
        t3 = (rows[3] - (v03 * rows[0] + v13 * rows[1])) * scale
        u2 = c33 * t2 - c23 * t3
        u3 = c22 * t3 - c23 * t2
        u0 = w0 - (v02 * u2 + v03 * u3)
        u1 = w1 - (v12 * u2 + v13 * u3)
        add = sum(jnp.where(sub == o + j, u, 0.0) for j, u in enumerate((u0, u1, u2, u3)))
        s = s - ((cols[0] * u0 + cols[1] * u1) + (cols[2] * u2 + cols[3] * u3))
        parts = [s[:g], (s[g] + add)[None], s[g + 1 :]]
        s = jnp.concatenate([part for part in parts if part.shape[0]], axis=0)
    return jnp.where(row == col, 2.0, 0.0) - s.reshape(n, n)


def kernel(
    nn, ns, nc, coords_ref, count_ref, owner_ref, corner_hbm, seg_ref, values_ref, out_ref, scale_ref,
    coords, count, owner, corner_ref,
    gathered, corner_all, corner_wide, values, partial, gram_in, gram_own, gram_all,
    summed, pair_in, rows_in, square, upper, local_sem, small_sem, z_send, z_recv, c_send, c_recv,
    h_send, h_recv, l_send, l_recv, g_send, g_recv, p_send, p_recv, s_send, s_recv,
):
    net, seg, corner = lax.axis_index("net"), lax.axis_index("seg"), lax.axis_index("corner")
    highs = nc // PAIR
    high, low = corner // PAIR, lax.rem(corner, PAIR)
    other_low = high * PAIR + 1 - low
    group = ns * nc
    pairs = group // PAIR
    slot = seg * nc + corner
    mine = seg * highs + high
    slots = values.shape[0]
    columns = corner_ref.shape[1]
    half = columns // 2
    held = gathered.shape[0] // nn
    chunk = held // nc
    net_rows = values.shape[1]

    def remote(src, dst, send, recv, **where):
        return pltpu.make_async_remote_copy(
            src_ref=src, dst_ref=dst, send_sem=send, recv_sem=recv, device_id=where, device_id_type=MESH
        )

    parts = local_sem.shape[0] - 1
    step = slots // parts
    loads = [
        pltpu.make_async_copy(
            values_ref.at[pl.ds(i * step, step)], values.at[pl.ds(i * step, step)], local_sem.at[i]
        )
        for i in range(parts)
    ]
    own_seg = pltpu.make_async_copy(seg_ref, gathered.at[pl.ds(net * held, held)], local_sem.at[parts])
    small = [
        pltpu.make_async_copy(source, to, small_sem.at[i])
        for i, (source, to) in enumerate(
            ((corner_hbm, corner_ref), (coords_ref, coords), (count_ref, count), (owner_ref, owner))
        )
    ]
    for copy in small:
        copy.start()
    own_seg.start()
    for load in loads:
        load.start()

    small[0].wait()
    barrier = pltpu.get_barrier_semaphore()
    for i in range(1, group):
        peer = lax.rem(slot + i, group)
        pl.semaphore_signal(
            barrier, inc=1, device_id={"seg": peer // nc, "corner": lax.rem(peer, nc)}, device_id_type=MESH
        )
    for i in range(1, nn):
        pl.semaphore_signal(barrier, inc=1, device_id={"net": lax.rem(net + i, nn)}, device_id_type=MESH)
    pl.semaphore_wait(barrier, group + nn - 2)

    def block(source, which):
        return pl.ds(source * held + which * chunk, chunk)

    sends = []

    def go(copy):
        copy.start()
        sends.append(copy)

    for i in range(1, nn):
        go(
            remote(
                seg_ref.at[pl.ds(corner * chunk, chunk)], gathered.at[block(net, corner)],
                z_send.at[i - 1], z_recv.at[i - 1], net=lax.rem(net + i, nn),
            )
        )
    for i in range(1, nc):
        go(
            remote(
                corner_ref, corner_all.at[corner], c_send.at[i - 1], c_recv.at[i - 1],
                corner=lax.rem(corner + i, nc),
            )
        )
    corner_all[pl.ds(corner, 1)] = corner_ref[...][None]
    corner_wide[...] = corner_ref[...].astype(jnp.float32).reshape(corner_wide.shape)

    def gram_of(source):
        rows = gathered[pl.ds(source * held, held)].reshape(-1, columns)
        left = gathered[pl.ds(source * held, held), :, pl.ds(pl.multiple_of(low * half, half), half)]
        return lax.dot_general(
            left.reshape(-1, half), rows, (((0,), (0,)), ((), ())), preferred_element_type=jnp.float32
        )

    own_seg.wait()
    gram_own[...] = gram_of(net)

    for i in range(1, nn):
        source = lax.rem(net - i + nn, nn)
        got = gathered.at[block(source, corner)]
        remote(got, got, z_send.at[i - 1], z_recv.at[i - 1], net=source).wait_recv()
        for j in range(1, highs):
            at = (i - 1) * (highs - 1) + j - 1
            go(
                remote(
                    got, got, h_send.at[at], h_recv.at[at], corner=lax.rem(high + j, highs) * PAIR + low
                )
            )
        at = (i - 1) * highs
        go(remote(got, got, l_send.at[at], l_recv.at[at], corner=other_low))
    for i in range(1, nn):
        source = lax.rem(net - i + nn, nn)
        for j in range(1, highs):
            at = (i - 1) * (highs - 1) + j - 1
            got = gathered.at[block(source, lax.rem(high - j + highs, highs) * PAIR + low)]
            remote(got, got, h_send.at[at], h_recv.at[at], corner=other_low).wait_recv()
            to = (i - 1) * highs + j
            go(remote(got, got, l_send.at[to], l_recv.at[to], corner=other_low))
    for i in range(1, nn):
        source = lax.rem(net - i + nn, nn)
        for j in range(highs):
            at = (i - 1) * highs + j
            got = gathered.at[block(source, lax.rem(high - j + highs, highs) * PAIR + 1 - low)]
            remote(got, got, l_send.at[at], l_recv.at[at], corner=other_low).wait_recv()
        gram_own[...] += gram_of(source)

    for j in range(1, ns):
        go(
            remote(
                gram_own, gram_in.at[j - 1], g_send.at[j - 1], g_recv.at[j - 1], seg=lax.rem(seg + j, ns)
            )
        )
    for load in loads + small[1:]:
        load.wait()

    corner_span, seg_span = corner_ref.shape[0] // CBLK, held * nn

    def tile(t):
        corner_rows = corner_wide[lax.rem(coords[0, t], corner_span)]
        seg_rows = gathered[lax.rem(coords[2, t], seg_span)].astype(jnp.float32)
        khatri = jnp.concatenate(
            [(corner_rows[a : a + 1, :] * seg_rows).astype(jnp.bfloat16) for a in range(CBLK)], axis=0
        )
        partial[t] = jnp.dot(values[t], khatri, preferred_element_type=jnp.float32)

    def four_tiles(i, carry):
        for j in range(4):
            tile(i * 4 + j)
        return carry

    lax.fori_loop(0, slots // 8, four_tiles, 0)

    total = gram_own[...]
    for j in range(1, ns):
        remote(
            gram_own, gram_in.at[j - 1], g_send.at[j - 1], g_recv.at[j - 1], seg=lax.rem(seg + j, ns)
        ).wait_recv()
        total = total + gram_in[j - 1]
    gram_all[pl.ds(low, 1)] = total[None]
    go(
        remote(
            gram_all.at[low], gram_all.at[low], g_send.at[ns - 1], g_recv.at[ns - 1], corner=other_low
        )
    )

    lax.fori_loop(slots // 8, slots // 4, four_tiles, 0)

    live = count[0]

    def add_up(q):
        block_of = owner[q]
        acc = jnp.zeros((net_rows, columns), jnp.float32)
        for t in range(slots):
            take = jnp.logical_and(coords[1, t] == block_of, t < live)
            acc = acc + jnp.where(take, partial[t], 0.0)
        return acc

    def pair_copy(h):
        return remote(
            summed.at[h * PAIR + 1 - low], pair_in.at[h], p_send.at[h], p_recv.at[h], corner=other_low
        )

    def give(h, carry):
        summed[pl.ds(h * PAIR + 1 - low, 1)] = add_up(h * PAIR + 1 - low)[None]
        pair_copy(h).start()
        return carry

    def keep(h, carry):
        summed[pl.ds(h * PAIR + low, 1)] = add_up(h * PAIR + low)[None]
        return carry

    lax.fori_loop(0, pairs, give, 0)
    lax.fori_loop(0, pairs, keep, 0)

    def row_copy(i):
        h = lax.rem(mine + i, pairs)
        return remote(
            summed.at[h * PAIR + low], rows_in.at[i - 1], s_send.at[i - 1], s_recv.at[i - 1],
            seg=h // highs, corner=lax.rem(h, highs) * PAIR + low,
        )

    def pass_on(i, carry):
        h = lax.rem(mine + i, pairs)
        got = pair_in.at[h]
        remote(got, got, p_send.at[h], p_recv.at[h], corner=other_low).wait_recv()
        at = h * PAIR + low
        summed[pl.ds(at, 1)] = summed[pl.ds(at, 1)] + pair_in[pl.ds(h, 1)]

        @pl.when(i < pairs)
        def _():
            row_copy(i).start()

        return carry

    lax.fori_loop(1, pairs + 1, pass_on, 0)

    for i in range(1, nc):
        remote(
            corner_ref, corner_all.at[lax.rem(corner - i + nc, nc)], c_send.at[i - 1], c_recv.at[i - 1],
            corner=lax.rem(corner + i, nc),
        ).wait_recv()
    remote(
        gram_all.at[low], gram_all.at[1 - low], g_send.at[ns - 1], g_recv.at[ns - 1], corner=other_low
    ).wait_recv()
    factor = corner_all[...].reshape(-1, columns)
    gram = lax.dot_general(factor, factor, (((0,), (0,)), ((), ())), preferred_element_type=jnp.float32)
    gram = gram * gram_all[...].reshape(columns, columns)
    row = lax.broadcasted_iota(jnp.int32, (columns, 1), 0)
    col = lax.broadcasted_iota(jnp.int32, (1, columns), 1)
    diag = jnp.where(row == col, gram, 0.0)
    scale_row = lax.rsqrt(jnp.sum(diag, axis=0, keepdims=True))
    scale_col = lax.rsqrt(jnp.sum(diag, axis=1, keepdims=True))
    gram = gram * scale_col * scale_row
    square[0] = gram[:half, :half]
    square[1] = gram[half:, half:]
    upper[0] = gram[:half, half:]

    def halves(h, carry):
        square[h] = invert(square[h])

        @pl.when(h == 0)
        def _():
            upper[1] = dot32(square[0], upper[0])
            square[1] = square[1] - dot32(upper[0], upper[1], ((0,), (0,)))

        return carry

    lax.fori_loop(0, 2, halves, 0)

    def take_rows(i, acc):
        row_copy(i).wait_recv()
        return acc + rows_in[i - 1]

    mttkrp = lax.fori_loop(1, pairs, take_rows, summed[slot]) * scale_row
    first, second = mttkrp[:, :half], mttkrp[:, half:]
    second = dot32(second - dot32(first, upper[1]), square[1])
    first = dot32(first - dot32(second, upper[0], ((1,), (1,))), square[0])
    out_ref[:, :half] = first
    out_ref[:, half:] = second
    scale_ref[...] = jnp.broadcast_to(scale_row, scale_ref.shape)

    for copy in sends:
        copy.wait_send()

    def end_pair(h, carry):
        pair_copy(h).wait_send()
        return carry

    def end_row(i, carry):
        row_copy(i).wait_send()
        return carry

    lax.fori_loop(0, pairs, end_pair, 0)
    lax.fori_loop(1, pairs, end_row, 0)


def body(tile_values, tile_coords, tile_count, owner_map, corner_factor, seg_factor):
    nn, ns, nc = lax.axis_size("net"), lax.axis_size("seg"), lax.axis_size("corner")
    slots, net_rows, depth = tile_values.shape
    columns = corner_factor.shape[1]
    width = depth // CBLK
    held = seg_factor.shape[0] // width
    group = ns * nc
    pairs, highs, half = group // PAIR, nc // PAIR, columns // 2
    vmem = pl.BlockSpec(memory_space=pltpu.VMEM)
    hbm = pl.BlockSpec(memory_space=pltpu.HBM)
    dma = lambda n: pltpu.SemaphoreType.DMA((max(n, 1),))
    f32, bf16 = jnp.float32, jnp.bfloat16
    rows, scale = pl.pallas_call(
        functools.partial(kernel, nn, ns, nc),
        out_shape=(jax.ShapeDtypeStruct((net_rows, columns), f32), jax.ShapeDtypeStruct((8, columns), f32)),
        in_specs=[hbm] * 6,
        out_specs=(vmem, vmem),
        scratch_shapes=[
            pltpu.SMEM((3, slots), jnp.int32),
            pltpu.SMEM(tile_count.shape, jnp.int32),
            pltpu.SMEM(owner_map.shape, jnp.int32),
            pltpu.VMEM(corner_factor.shape, bf16),
            pltpu.VMEM((nn * held, width, columns), bf16),
            pltpu.VMEM((nc,) + corner_factor.shape, bf16),
            pltpu.VMEM((corner_factor.shape[0] // CBLK, CBLK, columns), f32),
            pltpu.VMEM(tile_values.shape, bf16),
            pltpu.VMEM((slots, net_rows, columns), f32),
            pltpu.VMEM((max(ns - 1, 1), half, columns), f32),
            pltpu.VMEM((half, columns), f32),
            pltpu.VMEM((2, half, columns), f32),
            pltpu.VMEM((group, net_rows, columns), f32),
            pltpu.VMEM((pairs, net_rows, columns), f32),
            pltpu.VMEM((max(pairs - 1, 1), net_rows, columns), f32),
            pltpu.VMEM((2, half, half), f32),
            pltpu.VMEM((2, half, half), f32),
            dma(5), dma(4),
            dma(nn - 1), dma(nn - 1), dma(nc - 1), dma(nc - 1),
            dma((nn - 1) * (highs - 1)), dma((nn - 1) * (highs - 1)),
            dma((nn - 1) * highs), dma((nn - 1) * highs),
            dma(ns), dma(ns), dma(pairs), dma(pairs), dma(pairs - 1), dma(pairs - 1),
        ],
        compiler_params=pltpu.CompilerParams(
            collective_id=0, has_side_effects=True, vmem_limit_bytes=63 * 1024 * 1024
        ),
    )(
        tile_coords.T, tile_count, owner_map, corner_factor,
        seg_factor.reshape(held, width, columns), tile_values,
    )
    return (rows.reshape(-1, *scale.shape) * scale).reshape(rows.shape)


def solution(mesh):
    return jax.shard_map(
        body,
        mesh=mesh,
        in_specs=(
            P(("net", "seg", "corner"), None, None),
            P(("net", "seg", "corner"), None),
            P(("net", "seg", "corner")),
            P("net"),
            P("corner", None),
            P(("seg", "net"), None),
        ),
        out_specs=P(("net", "seg", "corner"), None),
        check_vma=False,
    )
```

```python
import functools

import jax
import jax.numpy as jnp
from jax import lax
from jax.experimental import pallas as pl
from jax.experimental.pallas import tpu as pltpu
from jax.sharding import PartitionSpec as P

CBLK = 8
MESH = pl.DeviceIdType.MESH
HIGH = lax.Precision.HIGHEST
PAIR = 2


def dot32(a, b, dims=((1,), (0,))):
    return lax.dot_general(a, b, (dims, ((), ())), precision=HIGH, preferred_element_type=jnp.float32)


def invert(s):
    n = s.shape[0]
    row = lax.broadcasted_iota(jnp.int32, (n, n), 0)
    col = lax.broadcasted_iota(jnp.int32, (n, n), 1)
    sub, lane = row[:8], col[:8]
    s = s.reshape(n // 8, 8, n)
    for k in range(0, n, 4):
        g, o = divmod(k, 8)
        cols = [jnp.broadcast_to(s[:, :, k + j : k + j + 1], s.shape) for j in range(4)]
        own = s[g]
        block = {
            (i, j): jnp.broadcast_to(cols[j][g][o + i : o + i + 1, :], (8, n))
            for i in range(4)
            for j in range(i, 4)
        }
        rows = [
            jnp.broadcast_to(own[o + i : o + i + 1, :], (8, n)) - jnp.where(lane == k + i, 1.0, 0.0)
            for i in range(4)
        ]
        scale = 1.0 / (block[0, 0] * block[1, 1] - block[0, 1] * block[0, 1])
        p00, p01, p11 = block[1, 1] * scale, -block[0, 1] * scale, block[0, 0] * scale
        v02 = p00 * block[0, 2] + p01 * block[1, 2]
        v03 = p00 * block[0, 3] + p01 * block[1, 3]
        v12 = p01 * block[0, 2] + p11 * block[1, 2]
        v13 = p01 * block[0, 3] + p11 * block[1, 3]
        c22 = block[2, 2] - (block[0, 2] * v02 + block[1, 2] * v12)
        c23 = block[2, 3] - (block[0, 2] * v03 + block[1, 2] * v13)
        c33 = block[3, 3] - (block[0, 3] * v03 + block[1, 3] * v13)
        scale = 1.0 / (c22 * c33 - c23 * c23)
        w0 = p00 * rows[0] + p01 * rows[1]
        w1 = p01 * rows[0] + p11 * rows[1]
        t2 = (rows[2] - (v02 * rows[0] + v12 * rows[1])) * scale
        t3 = (rows[3] - (v03 * rows[0] + v13 * rows[1])) * scale
        u2 = c33 * t2 - c23 * t3
        u3 = c22 * t3 - c23 * t2
        u0 = w0 - (v02 * u2 + v03 * u3)
        u1 = w1 - (v12 * u2 + v13 * u3)
        add = sum(jnp.where(sub == o + j, u, 0.0) for j, u in enumerate((u0, u1, u2, u3)))
        s = s - ((cols[0] * u0 + cols[1] * u1) + (cols[2] * u2 + cols[3] * u3))
        parts = [s[:g], (s[g] + add)[None], s[g + 1 :]]
        s = jnp.concatenate([part for part in parts if part.shape[0]], axis=0)
    return jnp.where(row == col, 2.0, 0.0) - s.reshape(n, n)


def kernel(
    nn, ns, nc, coords_ref, count_ref, owner_ref, corner_hbm, seg_ref, values_ref, out_ref, scale_ref,
    coords, count, owner, corner_ref,
    gathered, corner_all, corner_wide, values, partial, gram_in, gram_own, gram_all,
    summed, pair_in, rows_in, square, upper, local_sem, small_sem, z_send, z_recv, c_send, c_recv,
    h_send, h_recv, l_send, l_recv, g_send, g_recv, p_send, p_recv, s_send, s_recv,
):
    net, seg, corner = lax.axis_index("net"), lax.axis_index("seg"), lax.axis_index("corner")
    highs = nc // PAIR
    high, low = corner // PAIR, lax.rem(corner, PAIR)
    other_low = high * PAIR + 1 - low
    group = ns * nc
    pairs = group // PAIR
    slot = seg * nc + corner
    mine = seg * highs + high
    slots = values.shape[0]
    columns = corner_ref.shape[1]
    half = columns // 2
    held = gathered.shape[0] // nn
    chunk = held // nc
    net_rows = values.shape[1]

    def remote(src, dst, send, recv, **where):
        return pltpu.make_async_remote_copy(
            src_ref=src, dst_ref=dst, send_sem=send, recv_sem=recv, device_id=where, device_id_type=MESH
        )

    parts = local_sem.shape[0] - 1
    step = slots // parts
    loads = [
        pltpu.make_async_copy(
            values_ref.at[pl.ds(i * step, step)], values.at[pl.ds(i * step, step)], local_sem.at[i]
        )
        for i in range(parts)
    ]
    own_seg = pltpu.make_async_copy(seg_ref, gathered.at[pl.ds(net * held, held)], local_sem.at[parts])
    small = [
        pltpu.make_async_copy(source, to, small_sem.at[i])
        for i, (source, to) in enumerate(
            ((corner_hbm, corner_ref), (coords_ref, coords), (count_ref, count), (owner_ref, owner))
        )
    ]
    for copy in small:
        copy.start()
    own_seg.start()
    for load in loads:
        load.start()

    small[0].wait()
    barrier = pltpu.get_barrier_semaphore()
    for i in range(1, group):
        peer = lax.rem(slot + i, group)
        pl.semaphore_signal(
            barrier, inc=1, device_id={"seg": peer // nc, "corner": lax.rem(peer, nc)}, device_id_type=MESH
        )
    for i in range(1, nn):
        pl.semaphore_signal(barrier, inc=1, device_id={"net": lax.rem(net + i, nn)}, device_id_type=MESH)
    pl.semaphore_wait(barrier, group + nn - 2)

    def block(source, which):
        return pl.ds(source * held + which * chunk, chunk)

    sends = []

    def go(copy):
        copy.start()
        sends.append(copy)

    for i in range(1, nn):
        go(
            remote(
                seg_ref.at[pl.ds(corner * chunk, chunk)], gathered.at[block(net, corner)],
                z_send.at[i - 1], z_recv.at[i - 1], net=lax.rem(net + i, nn),
            )
        )
    for i in range(1, nc):
        go(
            remote(
                corner_ref, corner_all.at[corner], c_send.at[i - 1], c_recv.at[i - 1],
                corner=lax.rem(corner + i, nc),
            )
        )
    corner_all[pl.ds(corner, 1)] = corner_ref[...][None]
    corner_wide[...] = corner_ref[...].astype(jnp.float32).reshape(corner_wide.shape)

    def gram_of(source):
        rows = gathered[pl.ds(source * held, held)].reshape(-1, columns)
        left = gathered[pl.ds(source * held, held), :, pl.ds(pl.multiple_of(low * half, half), half)]
        return lax.dot_general(
            left.reshape(-1, half), rows, (((0,), (0,)), ((), ())), preferred_element_type=jnp.float32
        )

    own_seg.wait()
    gram_own[...] = gram_of(net)

    for i in range(1, nn):
        source = lax.rem(net - i + nn, nn)
        got = gathered.at[block(source, corner)]
        remote(got, got, z_send.at[i - 1], z_recv.at[i - 1], net=source).wait_recv()
        for j in range(1, highs):
            at = (i - 1) * (highs - 1) + j - 1
            go(
                remote(
                    got, got, h_send.at[at], h_recv.at[at], corner=lax.rem(high + j, highs) * PAIR + low
                )
            )
        at = (i - 1) * highs
        go(remote(got, got, l_send.at[at], l_recv.at[at], corner=other_low))
    for i in range(1, nn):
        source = lax.rem(net - i + nn, nn)
        for j in range(1, highs):
            at = (i - 1) * (highs - 1) + j - 1
            got = gathered.at[block(source, lax.rem(high - j + highs, highs) * PAIR + low)]
            remote(got, got, h_send.at[at], h_recv.at[at], corner=other_low).wait_recv()
            to = (i - 1) * highs + j
            go(remote(got, got, l_send.at[to], l_recv.at[to], corner=other_low))
    for i in range(1, nn):
        source = lax.rem(net - i + nn, nn)
        for j in range(highs):
            at = (i - 1) * highs + j
            got = gathered.at[block(source, lax.rem(high - j + highs, highs) * PAIR + 1 - low)]
            remote(got, got, l_send.at[at], l_recv.at[at], corner=other_low).wait_recv()
        gram_own[...] += gram_of(source)

    for j in range(1, ns):
        go(
            remote(
                gram_own, gram_in.at[j - 1], g_send.at[j - 1], g_recv.at[j - 1], seg=lax.rem(seg + j, ns)
            )
        )
    for load in loads + small[1:]:
        load.wait()

    corner_span, seg_span = corner_ref.shape[0] // CBLK, held * nn

    def tile(t):
        corner_rows = corner_wide[lax.rem(coords[0, t], corner_span)].astype(jnp.bfloat16)
        seg_rows = gathered[lax.rem(coords[2, t], seg_span)]
        khatri = jnp.concatenate(
            [corner_rows[a : a + 1, :] * seg_rows for a in range(CBLK)], axis=0
        )
        partial[t] = jnp.dot(values[t], khatri, preferred_element_type=jnp.float32)

    def four_tiles(i, carry):
        for j in range(4):
            tile(i * 4 + j)
        return carry

    lax.fori_loop(0, slots // 8, four_tiles, 0)

    total = gram_own[...]
    for j in range(1, ns):
        remote(
            gram_own, gram_in.at[j - 1], g_send.at[j - 1], g_recv.at[j - 1], seg=lax.rem(seg + j, ns)
        ).wait_recv()
        total = total + gram_in[j - 1]
    gram_all[pl.ds(low, 1)] = total[None]
    go(
        remote(
            gram_all.at[low], gram_all.at[low], g_send.at[ns - 1], g_recv.at[ns - 1], corner=other_low
        )
    )

    lax.fori_loop(slots // 8, slots // 4, four_tiles, 0)

    live = count[0]

    def add_up(q):
        block_of = owner[q]
        acc = jnp.zeros((net_rows, columns), jnp.float32)
        for t in range(slots):
            take = jnp.logical_and(coords[1, t] == block_of, t < live)
            acc = acc + jnp.where(take, partial[t], 0.0)
        return acc

    def pair_copy(h):
        return remote(
            summed.at[h * PAIR + 1 - low], pair_in.at[h], p_send.at[h], p_recv.at[h], corner=other_low
        )

    def give(h, carry):
        summed[pl.ds(h * PAIR + 1 - low, 1)] = add_up(h * PAIR + 1 - low)[None]
        pair_copy(h).start()
        return carry

    def keep(h, carry):
        summed[pl.ds(h * PAIR + low, 1)] = add_up(h * PAIR + low)[None]
        return carry

    lax.fori_loop(0, pairs, give, 0)
    lax.fori_loop(0, pairs, keep, 0)

    def row_copy(i):
        h = lax.rem(mine + i, pairs)
        return remote(
            summed.at[h * PAIR + low], rows_in.at[i - 1], s_send.at[i - 1], s_recv.at[i - 1],
            seg=h // highs, corner=lax.rem(h, highs) * PAIR + low,
        )

    def pass_on(i, carry):
        h = lax.rem(mine + i, pairs)
        got = pair_in.at[h]
        remote(got, got, p_send.at[h], p_recv.at[h], corner=other_low).wait_recv()
        at = h * PAIR + low
        summed[pl.ds(at, 1)] = summed[pl.ds(at, 1)] + pair_in[pl.ds(h, 1)]

        @pl.when(i < pairs)
        def _():
            row_copy(i).start()

        return carry

    lax.fori_loop(1, pairs + 1, pass_on, 0)

    for i in range(1, nc):
        remote(
            corner_ref, corner_all.at[lax.rem(corner - i + nc, nc)], c_send.at[i - 1], c_recv.at[i - 1],
            corner=lax.rem(corner + i, nc),
        ).wait_recv()
    remote(
        gram_all.at[low], gram_all.at[1 - low], g_send.at[ns - 1], g_recv.at[ns - 1], corner=other_low
    ).wait_recv()
    factor = corner_all[...].reshape(-1, columns)
    gram = lax.dot_general(factor, factor, (((0,), (0,)), ((), ())), preferred_element_type=jnp.float32)
    gram = gram * gram_all[...].reshape(columns, columns)
    row = lax.broadcasted_iota(jnp.int32, (columns, 1), 0)
    col = lax.broadcasted_iota(jnp.int32, (1, columns), 1)
    diag = jnp.where(row == col, gram, 0.0)
    scale_row = lax.rsqrt(jnp.sum(diag, axis=0, keepdims=True))
    scale_col = lax.rsqrt(jnp.sum(diag, axis=1, keepdims=True))
    gram = gram * scale_col * scale_row
    square[0] = gram[:half, :half]
    square[1] = gram[half:, half:]
    upper[0] = gram[:half, half:]

    def halves(h, carry):
        square[h] = invert(square[h])

        @pl.when(h == 0)
        def _():
            upper[1] = dot32(square[0], upper[0])
            square[1] = square[1] - dot32(upper[0], upper[1], ((0,), (0,)))

        return carry

    lax.fori_loop(0, 2, halves, 0)

    def take_rows(i, acc):
        row_copy(i).wait_recv()
        return acc + rows_in[i - 1]

    mttkrp = lax.fori_loop(1, pairs, take_rows, summed[slot]) * scale_row
    first, second = mttkrp[:, :half], mttkrp[:, half:]
    second = dot32(second - dot32(first, upper[1]), square[1])
    first = dot32(first - dot32(second, upper[0], ((1,), (1,))), square[0])
    out_ref[:, :half] = first
    out_ref[:, half:] = second
    scale_ref[...] = jnp.broadcast_to(scale_row, scale_ref.shape)

    for copy in sends:
        copy.wait_send()

    def end_pair(h, carry):
        pair_copy(h).wait_send()
        return carry

    def end_row(i, carry):
        row_copy(i).wait_send()
        return carry

    lax.fori_loop(0, pairs, end_pair, 0)
    lax.fori_loop(1, pairs, end_row, 0)


def body(tile_values, tile_coords, tile_count, owner_map, corner_factor, seg_factor):
    nn, ns, nc = lax.axis_size("net"), lax.axis_size("seg"), lax.axis_size("corner")
    slots, net_rows, depth = tile_values.shape
    columns = corner_factor.shape[1]
    width = depth // CBLK
    held = seg_factor.shape[0] // width
    group = ns * nc
    pairs, highs, half = group // PAIR, nc // PAIR, columns // 2
    vmem = pl.BlockSpec(memory_space=pltpu.VMEM)
    hbm = pl.BlockSpec(memory_space=pltpu.HBM)
    dma = lambda n: pltpu.SemaphoreType.DMA((max(n, 1),))
    f32, bf16 = jnp.float32, jnp.bfloat16
    rows, scale = pl.pallas_call(
        functools.partial(kernel, nn, ns, nc),
        out_shape=(jax.ShapeDtypeStruct((net_rows, columns), f32), jax.ShapeDtypeStruct((8, columns), f32)),
        in_specs=[hbm] * 6,
        out_specs=(vmem, vmem),
        scratch_shapes=[
            pltpu.SMEM((3, slots), jnp.int32),
            pltpu.SMEM(tile_count.shape, jnp.int32),
            pltpu.SMEM(owner_map.shape, jnp.int32),
            pltpu.VMEM(corner_factor.shape, bf16),
            pltpu.VMEM((nn * held, width, columns), bf16),
            pltpu.VMEM((nc,) + corner_factor.shape, bf16),
            pltpu.VMEM((corner_factor.shape[0] // CBLK, CBLK, columns), f32),
            pltpu.VMEM(tile_values.shape, bf16),
            pltpu.VMEM((slots, net_rows, columns), f32),
            pltpu.VMEM((max(ns - 1, 1), half, columns), f32),
            pltpu.VMEM((half, columns), f32),
            pltpu.VMEM((2, half, columns), f32),
            pltpu.VMEM((group, net_rows, columns), f32),
            pltpu.VMEM((pairs, net_rows, columns), f32),
            pltpu.VMEM((max(pairs - 1, 1), net_rows, columns), f32),
            pltpu.VMEM((2, half, half), f32),
            pltpu.VMEM((2, half, half), f32),
            dma(5), dma(4),
            dma(nn - 1), dma(nn - 1), dma(nc - 1), dma(nc - 1),
            dma((nn - 1) * (highs - 1)), dma((nn - 1) * (highs - 1)),
            dma((nn - 1) * highs), dma((nn - 1) * highs),
            dma(ns), dma(ns), dma(pairs), dma(pairs), dma(pairs - 1), dma(pairs - 1),
        ],
        compiler_params=pltpu.CompilerParams(
            collective_id=0, has_side_effects=True, vmem_limit_bytes=63 * 1024 * 1024
        ),
    )(
        tile_coords.T, tile_count, owner_map, corner_factor,
        seg_factor.reshape(held, width, columns), tile_values,
    )
    return (rows.reshape(-1, *scale.shape) * scale).reshape(rows.shape)


def solution(mesh):
    return jax.shard_map(
        body,
        mesh=mesh,
        in_specs=(
            P(("net", "seg", "corner"), None, None),
            P(("net", "seg", "corner"), None),
            P(("net", "seg", "corner")),
            P("net"),
            P("corner", None),
            P(("seg", "net"), None),
        ),
        out_specs=P(("net", "seg", "corner"), None),
        check_vma=False,
    )
```
